32 devices in a mesh: cfg: 2 (over x), tm: 16 (over z, y, core).
Axes of the slice: x: 2, y: 2, z: 4, core: 2. Of those that a mesh axis runs over, the one named last changes fastest.
Arguments:
- elemental: bfloat16 [32, 1024, 1024], P(('cfg', 'tm')), parts along dimension 0, may hold values from -0.1875 to 0.1875
- peramb: bfloat16 [32, 3, 1024, 1024], P(('cfg', 'tm')), parts along dimension 0, may hold values from -0.1875 to 0.1875
- seps: int32 [16, 3], P('tm'), may hold values from -2 to 2, as said below
Outputs:
- corr: float32 [32, 3], P(('cfg', 'tm')), parts along dimension 0
- pair: float32 [32, 3], P(('cfg', 'tm')), parts along dimension 0
The draws below stay inside these ranges and needn't reach their ends.
There are 2 independent parts, one for each index of `cfg`. The reference program is written for one: setup_inputs(seed, part) draws one part's arguments, and reference() takes and returns one part's arrays. A program takes and returns all parts, laid end to end along the dimension named above; an argument that names none is the same for every part. Nothing has to cross between parts.
Inputs may be any that keep to these rules, and one draw needn't show every extreme that they name: `seps`: every separation is nonzero; source slice 0 has separation 2 as its first pair and source slice 1 has -2.
All inputs are finite; a program needn't handle non-finite values.
Results may differ from the reference program's by a relative error of at most 0.0003.
Values may be sent and summed in bfloat16 or wider, within the bound.
A program may use at most 64 MiB of HBM per device.

```python
import jax
import jax.numpy as jnp
from jax import lax

NEV = 256
H = 2
SINK_SOURCE_PAIRS = 3
DILUTION_SPACE = 1024
TIME_EXTENT = 16


def draw_seps(key, part):
    magnitude = jax.random.randint(jax.random.fold_in(key, 11), (TIME_EXTENT, SINK_SOURCE_PAIRS), 1, H + 1)
    flips = jax.random.randint(jax.random.fold_in(key, 12), (TIME_EXTENT, SINK_SOURCE_PAIRS), 0, 2) * 2 - 1
    values = (magnitude * flips).astype(jnp.int32)
    values = values.at[0, 0].set(H).at[1, 0].set(-H)
    return values


def steps_of(stream_key, shape, pieces, low, high):
    factor_of = 1.0
    for axis_at, blocks in pieces:
        steps = jax.random.uniform(jax.random.fold_in(jax.random.fold_in(stream_key, 6), axis_at), (blocks,), jnp.float32, low / len(pieces), high / len(pieces))
        factor_of = factor_of * jnp.repeat(jnp.exp(steps), shape[axis_at] // blocks).reshape((-1,) + (1,) * (len(shape) - 1 - axis_at))
    return factor_of


def gaussian(rng, dims, deviation, reach, cuts=(), kind=jnp.bfloat16):
    level = steps_of(rng, dims, cuts, -0.22, 0.18) if cuts else 1.0
    drawn = jax.random.normal(rng, dims, jnp.float32) * deviation * level
    return jnp.minimum(jnp.maximum(drawn, -reach), reach).astype(kind)


def setup_inputs(seed: int = 0, part: int = 0) -> dict:
    streams_of = jax.random.split(jax.random.key(seed), 4)
    part_splits = jax.random.split(jax.random.fold_in(streams_of[3], part), 4)
    return {
        "elemental": gaussian(part_splits[0], (TIME_EXTENT, DILUTION_SPACE, DILUTION_SPACE), DILUTION_SPACE ** -0.5, 0.1875, ((0, 16),)),
        "peramb": gaussian(part_splits[1], (TIME_EXTENT, SINK_SOURCE_PAIRS, DILUTION_SPACE, DILUTION_SPACE), DILUTION_SPACE ** -0.5, 0.1875, ((0, 16),)),
        "seps": draw_seps(jax.random.fold_in(streams_of[3], 71), part),
    }


def reference(elemental, peramb, seps):
    block_rows = jnp.arange(DILUTION_SPACE, dtype=jnp.int32)
    sign = jnp.where(block_rows // NEV < 2, 1.0, -1.0).astype(jnp.float32)
    signs = (sign[:, None] * sign[None, :]).astype(jnp.bfloat16)

    def one_source(source):
        own = elemental[source]
        values = []
        for k in range(SINK_SOURCE_PAIRS):
            sink = jnp.mod(source + seps[source, k], TIME_EXTENT).astype(jnp.int32)
            tile = peramb[source, k]
            left = jnp.dot(elemental[sink], tile, preferred_element_type=jnp.float32)
            right = lax.dot_general(tile * signs, own, (((1,), (1,)), ((), ())), preferred_element_type=jnp.float32)
            values.append(jnp.sum(left * right))
        return jnp.stack(values)

    corr = lax.map(one_source, jnp.arange(TIME_EXTENT, dtype=jnp.int32))
    pair = corr * jnp.roll(corr, -1, axis=0)
    return corr, pair
```

```python
import functools

import jax
import jax.numpy as jnp
from jax import lax
from jax.experimental import pallas as pl
from jax.experimental.pallas import tpu as pltpu
from jax.sharding import PartitionSpec as P

NEV = 256
H = 2
CHUNKS = 16
WINDOW = 3
BLOCK = 256
NT = (((1,), (1,)), ((), ()))
MESH = pl.DeviceIdType.MESH


def kernel(
    peers, seps, e_hbm, p_hbm, corr_ref, pair_ref,
    es, p_v, z, buf, acc, mine, near, local_sem, send, recv, small_sem,
):
    count, width = p_v.shape[0], p_v.shape[1]
    chunk = width // CHUNKS
    block = min(BLOCK, width)
    steps = (width // block) * count

    me = lax.axis_index("tm")
    core = me % 2
    row = (me // 2) % 2
    across = me + 2 - 4 * row
    mate = me + 1 - 2 * core
    onward = (me + peers + 4 - 8 * row) % peers
    upstream = (me + peers - 4 + 8 * row) % peers
    before = (me + peers - 1) % peers
    after = (me + 1) % peers

    barrier = pltpu.get_barrier_semaphore()
    for peer in (across, mate, upstream, after):
        pl.semaphore_signal(barrier, inc=1, device_id={"tm": peer}, device_id_type=MESH)

    e_copy = pltpu.make_async_copy(e_hbm.at[0], es, local_sem.at[0])
    e_copy.start()
    p_copies = [
        pltpu.make_async_copy(p_hbm.at[0, k], p_v.at[k], local_sem.at[1 + k]) for k in range(count)
    ]
    for copy in p_copies:
        copy.start()
    pl.semaphore_wait(barrier, 4)

    def rows_of(j):
        return pl.ds(pl.multiple_of(j * chunk, chunk), chunk)

    def remote(src, slot, j, peer):
        return pltpu.make_async_remote_copy(
            src_ref=src.at[rows_of(j)],
            dst_ref=buf.at[slot, rows_of(j)],
            send_sem=send.at[slot, j],
            recv_sem=recv.at[slot, j],
            device_id={"tm": peer},
            device_id_type=MESH,
        )

    def across_copy(j):
        return remote(e_hbm.at[0], 0, j, across)

    def onward_copy(j):
        return remote(buf.at[0], 1, j, onward)

    def share_copy(j):
        return remote(buf.at[(row + core) % 2], 3, j, mate)

    mate_copy = pltpu.make_async_remote_copy(
        src_ref=e_hbm.at[0],
        dst_ref=buf.at[2],
        send_sem=small_sem.at[2],
        recv_sem=small_sem.at[3],
        device_id={"tm": mate},
        device_id_type=MESH,
    )

    for j in range(WINDOW):
        across_copy(j).start()
    mate_copy.start()

    acc[...] = jnp.zeros_like(acc)
    e_copy.wait()
    sign_row = jnp.where(lax.broadcasted_iota(jnp.int32, (1, width), 1) // NEV < 2, 1.0, -1.0)

    def flip(i, carry):
        at = pl.ds(pl.multiple_of(i * 128, 128), 128)
        es[at, :] = es[at, :] * sign_row.astype(jnp.bfloat16)
        return carry

    lax.fori_loop(0, width // 128, flip, 0)
    for copy in p_copies:
        copy.wait()

    def work(s):
        k = s % count
        first = pl.multiple_of((s // count) * block, block)
        at = pl.ds(first, block)
        index = first + lax.broadcasted_iota(jnp.int32, (block, 1), 0)
        sign = jnp.where(index // NEV < 2, 1.0, -1.0)
        g = lax.dot_general(p_v[k, at, :], es[...], NT, preferred_element_type=jnp.float32) * sign
        high = g.astype(jnp.bfloat16)
        low = (g - high.astype(jnp.float32)).astype(jnp.bfloat16)
        both = jnp.concatenate([high, low], axis=0)
        out = lax.dot_general(both, p_v[k], NT, preferred_element_type=jnp.float32)
        z[k, at, :] = out[:block] + out[block:]

    far = 2 * jnp.int32(1)
    offsets = (far - 2 * far * row, 2 * far * row - far, 1 - 2 * core, 2 * core - 1)

    def contract(slot, j):
        def part(i, totals):
            at = pl.ds(pl.multiple_of(j * chunk + i * 16, 16), 16)
            x = buf[slot, at, :].astype(jnp.float32)
            new = []
            for k in range(count):
                prod = x * z[k, at, :]
                new.append(totals[k] + (prod[:8] + prod[8:]))
            return tuple(new)

        zero = jnp.zeros((8, width), jnp.float32)
        totals = lax.fori_loop(0, chunk // 16, part, (zero,) * count, unroll=True)
        for k in range(count):
            acc[k] += jnp.where(seps[0, k] == offsets[slot], totals[k], 0.0)

    def step(j, carry):
        @pl.when(j < steps)
        def _():
            work(j)

        across_copy(j).wait_recv()
        onward_copy(j).start()
        across_copy(j).wait_send()

        @pl.when(j + WINDOW < CHUNKS)
        def _():
            across_copy(j + WINDOW).start()

        @pl.when(j >= 1)
        def _():
            onward_copy(j - 1).wait_recv()
            share_copy(j - 1).start()

        @pl.when(j == 2)
        def _():
            mate_copy.wait_recv()

        @pl.when(j >= 2)
        def _():
            contract(0, j - 2)
            contract(1, j - 2)
            contract(2, j - 2)
            share_copy(j - 2).wait_recv()
            contract(3, j - 2)

        return carry

    lax.fori_loop(0, CHUNKS, step, 0)
    last = CHUNKS - 1
    for slot in range(3):
        contract(slot, last - 1)
    contract(0, last)
    contract(2, last)
    share_copy(last - 1).wait_recv()
    contract(3, last - 1)
    onward_copy(last).wait_recv()
    share_copy(last).start()
    contract(1, last)
    share_copy(last).wait_recv()
    contract(3, last)

    lane = lax.broadcasted_iota(jnp.int32, (8, 128), 1)
    values = jnp.zeros((8, 128), jnp.float32)
    for k in range(count):
        values = jnp.where(lane == k, jnp.sum(acc[k]), values)
    mine[...] = values
    pass_on = pltpu.make_async_remote_copy(
        src_ref=mine,
        dst_ref=near,
        send_sem=small_sem.at[0],
        recv_sem=small_sem.at[1],
        device_id={"tm": before},
        device_id_type=MESH,
    )
    pass_on.start()

    def drain(j, carry):
        onward_copy(j).wait_send()
        share_copy(j).wait_send()
        return carry

    lax.fori_loop(0, CHUNKS, drain, 0)
    mate_copy.wait_send()
    corr_ref[...] = values[:1, :count]
    pass_on.wait()
    pair_ref[...] = values[:1, :count] * near[:1, :count]


def body(elemental, peramb, seps):
    peers = lax.axis_size("tm")
    count, width = peramb.shape[1], peramb.shape[2]
    small = jax.ShapeDtypeStruct((1, count), jnp.float32)
    return pl.pallas_call(
        functools.partial(kernel, peers),
        out_shape=(small, small),
        in_specs=[
            pl.BlockSpec(memory_space=pltpu.SMEM),
            pl.BlockSpec(memory_space=pl.ANY),
            pl.BlockSpec(memory_space=pl.ANY),
        ],
        out_specs=(pl.BlockSpec(memory_space=pltpu.VMEM),) * 2,
        scratch_shapes=[
            pltpu.VMEM((width, width), jnp.bfloat16),
            pltpu.VMEM((count, width, width), jnp.bfloat16),
            pltpu.VMEM((count, width, width), jnp.float32),
            pltpu.VMEM((4, width, width), jnp.bfloat16),
            pltpu.VMEM((count, 8, width), jnp.float32),
            pltpu.VMEM((8, 128), jnp.float32),
            pltpu.VMEM((8, 128), jnp.float32),
            pltpu.SemaphoreType.DMA((1 + count,)),
            pltpu.SemaphoreType.DMA((4, CHUNKS)),
            pltpu.SemaphoreType.DMA((4, CHUNKS)),
            pltpu.SemaphoreType.DMA((4,)),
        ],
        compiler_params=pltpu.CompilerParams(
            collective_id=0, has_side_effects=True, vmem_limit_bytes=60 * 1024 * 1024
        ),
        cost_estimate=pl.CostEstimate(
            flops=6 * count * width**3, bytes_accessed=2 * (1 + count) * width**2, transcendentals=0
        ),
        name="correlators",
    )(seps, elemental, peramb)


def solution(mesh):
    in_specs = (P(("cfg", "tm"), None, None), P(("cfg", "tm"), None, None, None), P("tm", None))
    out_specs = (P(("cfg", "tm"), None), P(("cfg", "tm"), None))
    return jax.shard_map(body, mesh=mesh, in_specs=in_specs, out_specs=out_specs, check_vma=False)
```

```python
import functools

import jax
import jax.numpy as jnp
from jax import lax
from jax.experimental import pallas as pl
from jax.experimental.pallas import tpu as pltpu
from jax.sharding import PartitionSpec as P

NEV = 256
H = 2
CHUNKS = 16
BLOCK = 256
NT = (((1,), (1,)), ((), ()))
MESH = pl.DeviceIdType.MESH


def kernel(
    peers, seps, e_hbm, p_hbm, corr_ref, pair_ref,
    es, p_v, z, buf, acc, mine, near, local_sem, send, recv, small_sem,
):
    count, width = p_v.shape[0], p_v.shape[1]
    chunk = width // CHUNKS
    block = min(BLOCK, width)
    steps = (width // block) * count

    me = lax.axis_index("tm")
    core = me % 2
    row = (me // 2) % 2
    across = me + 2 - 4 * row
    mate = me + 1 - 2 * core
    onward = (me + peers + 4 - 8 * row) % peers
    upstream = (me + peers - 4 + 8 * row) % peers
    before = (me + peers - 1) % peers
    after = (me + 1) % peers

    barrier = pltpu.get_barrier_semaphore()
    for peer in (across, mate, upstream, after):
        pl.semaphore_signal(barrier, inc=1, device_id={"tm": peer}, device_id_type=MESH)

    e_copy = pltpu.make_async_copy(e_hbm.at[0], es, local_sem.at[0])
    e_copy.start()
    p_copies = [
        pltpu.make_async_copy(p_hbm.at[0, k], p_v.at[k], local_sem.at[1 + k]) for k in range(count)
    ]
    for copy in p_copies:
        copy.start()
    pl.semaphore_wait(barrier, 4)

    def rows_of(j):
        return pl.ds(pl.multiple_of(j * chunk, chunk), chunk)

    def remote(src, slot, j, peer):
        return pltpu.make_async_remote_copy(
            src_ref=src.at[rows_of(j)],
            dst_ref=buf.at[slot, rows_of(j)],
            send_sem=send.at[slot, j],
            recv_sem=recv.at[slot, j],
            device_id={"tm": peer},
            device_id_type=MESH,
        )

    def across_copy(j):
        return remote(e_hbm.at[0], 0, j, across)

    def onward_copy(j):
        return remote(buf.at[0], 1, j, onward)

    def share_copy(j):
        return remote(buf.at[(row + core) % 2], 3, j, mate)

    mate_copy = pltpu.make_async_remote_copy(
        src_ref=e_hbm.at[0],
        dst_ref=buf.at[2],
        send_sem=small_sem.at[2],
        recv_sem=small_sem.at[3],
        device_id={"tm": mate},
        device_id_type=MESH,
    )

    def launch(j, carry):
        across_copy(j).start()
        return carry

    lax.fori_loop(0, CHUNKS, launch, 0)
    mate_copy.start()

    acc[...] = jnp.zeros_like(acc)
    e_copy.wait()
    sign_row = jnp.where(lax.broadcasted_iota(jnp.int32, (1, width), 1) // NEV < 2, 1.0, -1.0)

    def flip(i, carry):
        at = pl.ds(pl.multiple_of(i * 128, 128), 128)
        es[at, :] = es[at, :] * sign_row.astype(jnp.bfloat16)
        return carry

    lax.fori_loop(0, width // 128, flip, 0)
    def work(s):
        k = s % count
        first = pl.multiple_of((s // count) * block, block)
        at = pl.ds(first, block)
        index = first + lax.broadcasted_iota(jnp.int32, (block, 1), 0)
        sign = jnp.where(index // NEV < 2, 1.0, -1.0)
        g = lax.dot_general(p_v[k, at, :], es[...], NT, preferred_element_type=jnp.float32) * sign
        high = g.astype(jnp.bfloat16)
        low = (g - high.astype(jnp.float32)).astype(jnp.bfloat16)
        both = jnp.concatenate([high, low], axis=0)
        out = lax.dot_general(both, p_v[k], NT, preferred_element_type=jnp.float32)
        z[k, at, :] = out[:block] + out[block:]

    offsets = (H - 2 * H * row, 2 * H * row - H, 1 - 2 * core, 2 * core - 1)

    def contract(slot, j):
        def part(i, totals):
            at = pl.ds(pl.multiple_of(j * chunk + i * 16, 16), 16)
            x = buf[slot, at, :].astype(jnp.float32)
            new = []
            for k in range(count):
                prod = x * z[k, at, :]
                new.append(totals[k] + (prod[:8] + prod[8:]))
            return tuple(new)

        zero = jnp.zeros((8, width), jnp.float32)
        totals = lax.fori_loop(0, chunk // 16, part, (zero,) * count, unroll=True)
        for k in range(count):
            acc[k] += jnp.where(seps[0, k] == offsets[slot], totals[k], 0.0)

    def forward(j):
        across_copy(j).wait_recv()
        onward_copy(j).start()

    def share(j):
        onward_copy(j).wait_recv()
        share_copy(j).start()

    def finish(j):
        share_copy(j).wait_recv()
        for slot in range(4):
            contract(slot, j)

    def step(j, carry):
        forward(j)

        @pl.when(j >= 2)
        def _():
            share(j - 2)

        @pl.when(j == 0)
        def _():
            for copy in p_copies:
                copy.wait()

        @pl.when(j < steps)
        def _():
            work(j)

        @pl.when(j == 3)
        def _():
            mate_copy.wait_recv()

        @pl.when(j >= 3)
        def _():
            finish(j - 3)

        return carry

    lax.fori_loop(0, CHUNKS, step, 0)
    last = CHUNKS - 1
    share(last - 1)
    finish(last - 2)
    contract(0, last - 1)
    contract(1, last - 1)
    contract(2, last - 1)
    contract(0, last)
    contract(2, last)
    share(last)
    contract(1, last)
    share_copy(last - 1).wait_recv()
    contract(3, last - 1)
    share_copy(last).wait_recv()
    contract(3, last)

    lane = lax.broadcasted_iota(jnp.int32, (8, 128), 1)
    values = jnp.zeros((8, 128), jnp.float32)
    for k in range(count):
        values = jnp.where(lane == k, jnp.sum(acc[k]), values)
    mine[...] = values
    pass_on = pltpu.make_async_remote_copy(
        src_ref=mine,
        dst_ref=near,
        send_sem=small_sem.at[0],
        recv_sem=small_sem.at[1],
        device_id={"tm": before},
        device_id_type=MESH,
    )
    pass_on.start()

    def drain(j, carry):
        across_copy(j).wait_send()
        onward_copy(j).wait_send()
        share_copy(j).wait_send()
        return carry

    lax.fori_loop(0, CHUNKS, drain, 0)
    mate_copy.wait_send()
    corr_ref[...] = values[:1, :count]
    pass_on.wait()
    pair_ref[...] = values[:1, :count] * near[:1, :count]


def body(elemental, peramb, seps):
    peers = lax.axis_size("tm")
    count, width = peramb.shape[1], peramb.shape[2]
    small = jax.ShapeDtypeStruct((1, count), jnp.float32)
    return pl.pallas_call(
        functools.partial(kernel, peers),
        out_shape=(small, small),
        in_specs=[
            pl.BlockSpec(memory_space=pltpu.SMEM),
            pl.BlockSpec(memory_space=pl.ANY),
            pl.BlockSpec(memory_space=pl.ANY),
        ],
        out_specs=(pl.BlockSpec(memory_space=pltpu.VMEM),) * 2,
        scratch_shapes=[
            pltpu.VMEM((width, width), jnp.bfloat16),
            pltpu.VMEM((count, width, width), jnp.bfloat16),
            pltpu.VMEM((count, width, width), jnp.float32),
            pltpu.VMEM((4, width, width), jnp.bfloat16),
            pltpu.VMEM((count, 8, width), jnp.float32),
            pltpu.VMEM((8, 128), jnp.float32),
            pltpu.VMEM((8, 128), jnp.float32),
            pltpu.SemaphoreType.DMA((1 + count,)),
            pltpu.SemaphoreType.DMA((4, CHUNKS)),
            pltpu.SemaphoreType.DMA((4, CHUNKS)),
            pltpu.SemaphoreType.DMA((4,)),
        ],
        compiler_params=pltpu.CompilerParams(
            collective_id=0, has_side_effects=True, vmem_limit_bytes=60 * 1024 * 1024
        ),
        cost_estimate=pl.CostEstimate(
            flops=6 * count * width**3, bytes_accessed=2 * (1 + count) * width**2, transcendentals=0
        ),
        name="correlators",
    )(seps, elemental, peramb)


def solution(mesh):
    in_specs = (P(("cfg", "tm"), None, None), P(("cfg", "tm"), None, None, None), P("tm", None))
    out_specs = (P(("cfg", "tm"), None), P(("cfg", "tm"), None))
    return jax.shard_map(body, mesh=mesh, in_specs=in_specs, out_specs=out_specs, check_vma=False)
```

```python
import functools

import jax
import jax.numpy as jnp
from jax import lax
from jax.experimental import pallas as pl
from jax.experimental.pallas import tpu as pltpu
from jax.sharding import PartitionSpec as P

NEV = 256
H = 2
CHUNKS = 16
BLOCK = 256
NT = (((1,), (1,)), ((), ()))
MESH = pl.DeviceIdType.MESH


def kernel(
    peers, seps, e_hbm, p_hbm, out_ref,
    es, p_v, z, buf, acc, mine, near, local_sem, send, recv, small_sem,
):
    count, width = p_v.shape[0], p_v.shape[1]
    chunk = width // CHUNKS
    block = min(BLOCK, width)
    steps = (width // block) * count

    me = lax.axis_index("tm")
    core = me % 2
    row = (me // 2) % 2
    across = me + 2 - 4 * row
    mate = me + 1 - 2 * core
    onward = (me + peers + 4 - 8 * row) % peers
    upstream = (me + peers - 4 + 8 * row) % peers
    before = (me + peers - 1) % peers
    after = (me + 1) % peers

    barrier = pltpu.get_barrier_semaphore()
    for peer in (across, mate, upstream, after):
        pl.semaphore_signal(barrier, inc=1, device_id={"tm": peer}, device_id_type=MESH)

    e_copy = pltpu.make_async_copy(e_hbm.at[0], es, local_sem.at[0])
    p_copies = [
        pltpu.make_async_copy(p_hbm.at[0, k], p_v.at[k], local_sem.at[1 + k]) for k in range(count)
    ]
    pl.semaphore_wait(barrier, 4)

    def rows_of(j):
        return pl.ds(pl.multiple_of(j * chunk, chunk), chunk)

    def remote(src, slot, j, peer):
        return pltpu.make_async_remote_copy(
            src_ref=src.at[rows_of(j)],
            dst_ref=buf.at[slot, rows_of(j)],
            send_sem=send.at[slot, j],
            recv_sem=recv.at[slot, j],
            device_id={"tm": peer},
            device_id_type=MESH,
        )

    def across_copy(j):
        return remote(e_hbm.at[0], 0, j, across)

    def onward_copy(j):
        return remote(buf.at[0], 1, j, onward)

    def share_copy(j):
        return remote(buf.at[(row + core) % 2], 3, j, mate)

    mate_copy = pltpu.make_async_remote_copy(
        src_ref=e_hbm.at[0],
        dst_ref=buf.at[2],
        send_sem=small_sem.at[2],
        recv_sem=small_sem.at[3],
        device_id={"tm": mate},
        device_id_type=MESH,
    )

    def forward(j):
        across_copy(j).wait_recv()
        onward_copy(j).start()

    def launch(j, carry):
        across_copy(j).start()
        return carry

    lax.fori_loop(0, CHUNKS, launch, 0)
    mate_copy.start()
    e_copy.start()
    for copy in p_copies:
        copy.start()

    acc[...] = jnp.zeros_like(acc)
    forward(0)
    e_copy.wait()
    sign_row = jnp.where(lax.broadcasted_iota(jnp.int32, (1, width), 1) // NEV < 2, 1.0, -1.0)

    def flip(i, carry):
        at = pl.ds(pl.multiple_of(i * 128, 128), 128)
        es[at, :] = es[at, :] * sign_row.astype(jnp.bfloat16)
        return carry

    lax.fori_loop(0, width // 128, flip, 0)
    def work(s):
        k = s % count
        first = pl.multiple_of((s // count) * block, block)
        at = pl.ds(first, block)
        index = first + lax.broadcasted_iota(jnp.int32, (block, 1), 0)
        sign = jnp.where(index // NEV < 2, 1.0, -1.0)
        g = lax.dot_general(p_v[k, at, :], es[...], NT, preferred_element_type=jnp.float32) * sign
        high = g.astype(jnp.bfloat16)
        low = (g - high.astype(jnp.float32)).astype(jnp.bfloat16)
        both = jnp.concatenate([high, low], axis=0)
        out = lax.dot_general(both, p_v[k], NT, preferred_element_type=jnp.float32)
        z[k, at, :] = out[:block] + out[block:]

    offsets = (H - 2 * H * row, 2 * H * row - H, 1 - 2 * core, 2 * core - 1)

    def contract(slot, j):
        def part(i, totals):
            at = pl.ds(pl.multiple_of(j * chunk + i * 16, 16), 16)
            x = buf[slot, at, :].astype(jnp.float32)
            new = []
            for k in range(count):
                prod = x * z[k, at, :]
                new.append(totals[k] + (prod[:8] + prod[8:]))
            return tuple(new)

        zero = jnp.zeros((8, width), jnp.float32)
        totals = lax.fori_loop(0, chunk // 16, part, (zero,) * count, unroll=True)
        for k in range(count):
            acc[k] += jnp.where(seps[0, k] == offsets[slot], totals[k], 0.0)

    def share(j):
        onward_copy(j).wait_recv()
        share_copy(j).start()

    def finish(j):
        share_copy(j).wait_recv()
        for slot in range(4):
            contract(slot, j)

    def step(j, carry):
        @pl.when(j >= 1)
        def _():
            forward(j)

        @pl.when(j >= 2)
        def _():
            share(j - 2)

        @pl.when(j == 0)
        def _():
            for copy in p_copies:
                copy.wait()

        @pl.when(j < steps)
        def _():
            work(j)

        @pl.when(j == 3)
        def _():
            mate_copy.wait_recv()

        @pl.when(j >= 3)
        def _():
            finish(j - 3)

        return carry

    lax.fori_loop(0, CHUNKS, step, 0)
    last = CHUNKS - 1
    share(last - 1)
    finish(last - 2)
    contract(0, last - 1)
    contract(1, last - 1)
    contract(2, last - 1)
    contract(0, last)
    contract(2, last)
    share(last)
    contract(1, last)
    share_copy(last - 1).wait_recv()
    contract(3, last - 1)
    share_copy(last).wait_recv()
    contract(3, last)

    lane = lax.broadcasted_iota(jnp.int32, (8, 128), 1)
    values = jnp.zeros((8, 128), jnp.float32)
    for k in range(count):
        values = jnp.where(lane == k, jnp.sum(acc[k]), values)
    mine[...] = values
    pass_on = pltpu.make_async_remote_copy(
        src_ref=mine,
        dst_ref=near,
        send_sem=small_sem.at[0],
        recv_sem=small_sem.at[1],
        device_id={"tm": before},
        device_id_type=MESH,
    )
    pass_on.start()

    def drain(j, carry):
        across_copy(j).wait_send()
        onward_copy(j).wait_send()
        share_copy(j).wait_send()
        return carry

    lax.fori_loop(0, CHUNKS, drain, 0)
    mate_copy.wait_send()
    out_ref[0:1, :] = values[:1, :count]
    pass_on.wait()
    out_ref[1:2, :] = values[:1, :count] * near[:1, :count]


def body(elemental, peramb, seps):
    peers = lax.axis_size("tm")
    count, width = peramb.shape[1], peramb.shape[2]
    out = pl.pallas_call(
        functools.partial(kernel, peers),
        out_shape=jax.ShapeDtypeStruct((2, count), jnp.float32),
        in_specs=[
            pl.BlockSpec(memory_space=pltpu.SMEM),
            pl.BlockSpec(memory_space=pl.ANY),
            pl.BlockSpec(memory_space=pl.ANY),
        ],
        out_specs=pl.BlockSpec(memory_space=pltpu.VMEM),
        scratch_shapes=[
            pltpu.VMEM((width, width), jnp.bfloat16),
            pltpu.VMEM((count, width, width), jnp.bfloat16),
            pltpu.VMEM((count, width, width), jnp.float32),
            pltpu.VMEM((4, width, width), jnp.bfloat16),
            pltpu.VMEM((count, 8, width), jnp.float32),
            pltpu.VMEM((8, 128), jnp.float32),
            pltpu.VMEM((8, 128), jnp.float32),
            pltpu.SemaphoreType.DMA((1 + count,)),
            pltpu.SemaphoreType.DMA((4, CHUNKS)),
            pltpu.SemaphoreType.DMA((4, CHUNKS)),
            pltpu.SemaphoreType.DMA((4,)),
        ],
        compiler_params=pltpu.CompilerParams(
            collective_id=0, has_side_effects=True, vmem_limit_bytes=60 * 1024 * 1024
        ),
        cost_estimate=pl.CostEstimate(
            flops=6 * count * width**3, bytes_accessed=2 * (1 + count) * width**2, transcendentals=0
        ),
        name="correlators",
    )(seps, elemental, peramb)
    return out[:1], out[1:]


def solution(mesh):
    in_specs = (P(("cfg", "tm"), None, None), P(("cfg", "tm"), None, None, None), P("tm", None))
    out_specs = (P(("cfg", "tm"), None), P(("cfg", "tm"), None))
    return jax.shard_map(body, mesh=mesh, in_specs=in_specs, out_specs=out_specs, check_vma=False)
```

```python
import functools

import jax
import jax.numpy as jnp
from jax import lax
from jax.experimental import pallas as pl
from jax.experimental.pallas import tpu as pltpu
from jax.sharding import PartitionSpec as P

NEV = 256
H = 2
CHUNKS = 16
BLOCK = 256
NT = (((1,), (1,)), ((), ()))
MESH = pl.DeviceIdType.MESH


def kernel(
    peers, seps, e_hbm, p_hbm, out_ref,
    es, p_v, z, buf, acc, mine, near, local_sem, send, recv, small_sem,
):
    count, width = p_v.shape[0], p_v.shape[1]
    chunk = width // CHUNKS
    block = min(BLOCK, width)
    steps = (width // block) * count

    me = lax.axis_index("tm")
    core = me % 2
    row = (me // 2) % 2
    across = me + 2 - 4 * row
    mate = me + 1 - 2 * core
    onward = (me + peers + 4 - 8 * row) % peers
    upstream = (me + peers - 4 + 8 * row) % peers
    before = (me + peers - 1) % peers
    after = (me + 1) % peers

    barrier = pltpu.get_barrier_semaphore()
    for peer in (across, mate, upstream, after):
        pl.semaphore_signal(barrier, inc=1, device_id={"tm": peer}, device_id_type=MESH)

    e_copy = pltpu.make_async_copy(e_hbm.at[0], es, local_sem.at[0])
    p_copies = [
        pltpu.make_async_copy(p_hbm.at[0, k], p_v.at[k], local_sem.at[1 + k]) for k in range(count)
    ]
    pl.semaphore_wait(barrier, 4)

    def rows_of(j):
        return pl.ds(pl.multiple_of(j * chunk, chunk), chunk)

    def remote(src, slot, j, peer):
        return pltpu.make_async_remote_copy(
            src_ref=src.at[rows_of(j)],
            dst_ref=buf.at[slot, rows_of(j)],
            send_sem=send.at[slot, j],
            recv_sem=recv.at[slot, j],
            device_id={"tm": peer},
            device_id_type=MESH,
        )

    def across_copy(j):
        return remote(e_hbm.at[0], 0, j, across)

    def onward_copy(j):
        return remote(buf.at[0], 1, j, onward)

    def share_copy(j):
        return remote(buf.at[(row + core) % 2], 3, j, mate)

    mate_copy = pltpu.make_async_remote_copy(
        src_ref=e_hbm.at[0],
        dst_ref=buf.at[2],
        send_sem=small_sem.at[2],
        recv_sem=small_sem.at[3],
        device_id={"tm": mate},
        device_id_type=MESH,
    )

    def forward(j):
        across_copy(j).wait_recv()
        onward_copy(j).start()

    def launch(j, carry):
        across_copy(j).start()
        return carry

    lax.fori_loop(0, CHUNKS, launch, 0)
    e_copy.start()
    for copy in p_copies:
        copy.start()

    acc[...] = jnp.zeros_like(acc)
    forward(0)
    mate_copy.start()
    e_copy.wait()
    sign_row = jnp.where(lax.broadcasted_iota(jnp.int32, (1, width), 1) // NEV < 2, 1.0, -1.0)

    def flip(i, carry):
        at = pl.ds(pl.multiple_of(i * 128, 128), 128)
        es[at, :] = es[at, :] * sign_row.astype(jnp.bfloat16)
        return carry

    lax.fori_loop(0, width // 128, flip, 0)
    def work(s):
        k = s % count
        first = pl.multiple_of((s // count) * block, block)
        at = pl.ds(first, block)
        index = first + lax.broadcasted_iota(jnp.int32, (block, 1), 0)
        sign = jnp.where(index // NEV < 2, 1.0, -1.0)
        g = lax.dot_general(p_v[k, at, :], es[...], NT, preferred_element_type=jnp.float32) * sign
        high = g.astype(jnp.bfloat16)
        low = (g - high.astype(jnp.float32)).astype(jnp.bfloat16)
        both = jnp.concatenate([high, low], axis=0)
        out = lax.dot_general(both, p_v[k], NT, preferred_element_type=jnp.float32)
        z[k, at, :] = out[:block] + out[block:]

    offsets = (H - 2 * H * row, 2 * H * row - H, 1 - 2 * core, 2 * core - 1)

    def contract(slot, j):
        def part(i, totals):
            at = pl.ds(pl.multiple_of(j * chunk + i * 16, 16), 16)
            x = buf[slot, at, :].astype(jnp.float32)
            new = []
            for k in range(count):
                prod = x * z[k, at, :]
                new.append(totals[k] + (prod[:8] + prod[8:]))
            return tuple(new)

        zero = jnp.zeros((8, width), jnp.float32)
        totals = lax.fori_loop(0, chunk // 16, part, (zero,) * count, unroll=True)
        for k in range(count):
            acc[k] += jnp.where(seps[0, k] == offsets[slot], totals[k], 0.0)

    def share(j):
        onward_copy(j).wait_recv()
        share_copy(j).start()

    def finish(j):
        share_copy(j).wait_recv()
        for slot in range(4):
            contract(slot, j)

    def step(j, carry):
        @pl.when(j >= 1)
        def _():
            forward(j)

        @pl.when(j >= 2)
        def _():
            share(j - 2)

        @pl.when(j == 0)
        def _():
            for copy in p_copies:
                copy.wait()

        @pl.when(j < steps)
        def _():
            work(j)

        @pl.when(j == 3)
        def _():
            mate_copy.wait_recv()

        @pl.when(j >= 3)
        def _():
            finish(j - 3)

        return carry

    lax.fori_loop(0, CHUNKS, step, 0)
    last = CHUNKS - 1
    share(last - 1)
    finish(last - 2)
    contract(0, last - 1)
    contract(1, last - 1)
    contract(2, last - 1)
    contract(0, last)
    contract(2, last)
    share(last)
    contract(1, last)
    share_copy(last - 1).wait_recv()
    contract(3, last - 1)
    share_copy(last).wait_recv()
    contract(3, last)

    lane = lax.broadcasted_iota(jnp.int32, (8, 128), 1)
    values = jnp.zeros((8, 128), jnp.float32)
    for k in range(count):
        values = jnp.where(lane == k, jnp.sum(acc[k], axis=(0, 1), keepdims=True), values)
    mine[...] = values
    pass_on = pltpu.make_async_remote_copy(
        src_ref=mine,
        dst_ref=near,
        send_sem=small_sem.at[0],
        recv_sem=small_sem.at[1],
        device_id={"tm": before},
        device_id_type=MESH,
    )
    pass_on.start()

    def drain(j, carry):
        across_copy(j).wait_send()
        onward_copy(j).wait_send()
        share_copy(j).wait_send()
        return carry

    lax.fori_loop(0, CHUNKS, drain, 0)
    mate_copy.wait_send()
    out_ref[0:1, :] = values[:1, :count]
    pass_on.wait()
    out_ref[1:2, :] = values[:1, :count] * near[:1, :count]


def body(elemental, peramb, seps):
    peers = lax.axis_size("tm")
    count, width = peramb.shape[1], peramb.shape[2]
    out = pl.pallas_call(
        functools.partial(kernel, peers),
        out_shape=jax.ShapeDtypeStruct((2, count), jnp.float32),
        in_specs=[
            pl.BlockSpec(memory_space=pltpu.SMEM),
            pl.BlockSpec(memory_space=pl.ANY),
            pl.BlockSpec(memory_space=pl.ANY),
        ],
        out_specs=pl.BlockSpec(memory_space=pltpu.VMEM),
        scratch_shapes=[
            pltpu.VMEM((width, width), jnp.bfloat16),
            pltpu.VMEM((count, width, width), jnp.bfloat16),
            pltpu.VMEM((count, width, width), jnp.float32),
            pltpu.VMEM((4, width, width), jnp.bfloat16),
            pltpu.VMEM((count, 8, width), jnp.float32),
            pltpu.VMEM((8, 128), jnp.float32),
            pltpu.VMEM((8, 128), jnp.float32),
            pltpu.SemaphoreType.DMA((1 + count,)),
            pltpu.SemaphoreType.DMA((4, CHUNKS)),
            pltpu.SemaphoreType.DMA((4, CHUNKS)),
            pltpu.SemaphoreType.DMA((4,)),
        ],
        compiler_params=pltpu.CompilerParams(
            collective_id=0, has_side_effects=True, vmem_limit_bytes=60 * 1024 * 1024
        ),
        cost_estimate=pl.CostEstimate(
            flops=6 * count * width**3, bytes_accessed=2 * (1 + count) * width**2, transcendentals=0
        ),
        name="correlators",
    )(seps, elemental, peramb)
    return out[:1], out[1:]


def solution(mesh):
    in_specs = (P(("cfg", "tm"), None, None), P(("cfg", "tm"), None, None, None), P("tm", None))
    out_specs = (P(("cfg", "tm"), None), P(("cfg", "tm"), None))
    return jax.shard_map(body, mesh=mesh, in_specs=in_specs, out_specs=out_specs, check_vma=False)
```
